512 devices in a mesh: dp: 2 (over core), row: 16 (over y, z_hi), col: 16 (over x, z_lo).
Axes of the slice: x: 4, y: 8, z: 8 (z_hi: 2, z_lo: 4; z = z_hi * 4 + z_lo), core: 2. Of those that a mesh axis runs over, the one named last changes fastest.
Arguments:
- patches: bfloat16 [1536, 6144], P(('dp', 'col'), 'row'), may hold values from -250 to 250
- norm_gain: float32 [6144], P('row'), may hold values from 0.1 to 1.9
- w_in: bfloat16 [6144, 12288], P('row', 'col'), may hold values from -0.078125 to 0.078125
- w_out: bfloat16 [12288, 6144], P('col', 'row'), may hold values from -0.0546875 to 0.0546875
- out_grad: bfloat16 [1536, 6144], P(('dp', 'col'), 'row'), may hold values from -3 to 3
Outputs:
- branch: bfloat16 [1536, 6144], P(('dp', 'col'), 'row')
- grad_patches: bfloat16 [1536, 6144], P(('dp', 'col'), 'row')
- grad_w_in: float32 [6144, 12288], P('row', 'col')
- grad_w_out: float32 [12288, 6144], P('col', 'row')
- grad_gain: float32 [6144], P('row')
The draws below stay inside these ranges and needn't reach their ends.
All inputs are finite; a program needn't handle non-finite values.
Results may differ from the reference program's by a relative error of at most 0.034.
Values may be sent and summed in bfloat16 or wider, within the bound.
No kernel may reach another device: no remote copies, remote signals or barrier semaphores. Data moves between devices by JAX's collectives and lax.ppermute only.
A program may use at most 64 MiB of HBM per device.

```python
import jax
import jax.numpy as jnp
from jax import lax

D = 6144
FF_WIN = 12288
TOK_REP = 768
TOKENS = 1536
N_DP = 2
N_ROW = 16
N_COL = 16


def draw_patches(key, part):
    key = jax.random.fold_in(key, 11)
    keys = jax.random.split(key, 3)
    columns = 3.0 ** (jnp.arange(D, dtype=jnp.float32) / D)
    columns = columns * jnp.exp(jax.random.uniform(keys[1], (D,), jnp.float32, -0.7, 0.7))
    rows = jnp.exp(jax.random.uniform(keys[2], (TOKENS, 1), jnp.float32, 0.0, 2.302585))
    base = jnp.clip(jax.random.normal(keys[0], (TOKENS, D), jnp.float32), -4.0, 4.0)
    return (base * rows * columns).astype(jnp.bfloat16)


def level_of(stream_key, extent, cuts, smallest, largest):
    factor_of = 1.0
    for position, parts in cuts:
        draws = jax.random.uniform(jax.random.fold_in(jax.random.fold_in(stream_key, 6), position), (parts,), jnp.float32, smallest / len(cuts), largest / len(cuts))
        factor_of = factor_of * jnp.repeat(jnp.exp(draws), extent[position] // parts).reshape((-1,) + (1,) * (len(extent) - 1 - position))
    return factor_of


def bell_draw(own_key, dims, scale, bound, cuts=(), kind=jnp.bfloat16):
    drawn = scale * jax.random.normal(own_key, dims, jnp.float32)
    if cuts:
        drawn = drawn * level_of(own_key, dims, cuts, -0.22, 0.18)
    return jnp.clip(drawn, -bound, bound).astype(kind)


def setup_inputs(seed: int = 0) -> dict:
    splits = jax.random.split(jax.random.key(seed), 6)
    return {
        "patches": draw_patches(jax.random.fold_in(splits[5], 71), 0),
        "norm_gain": jnp.clip(1.0 + 0.18 * jax.random.normal(splits[1], (D,), jnp.float32), 0.1, 1.9),
        "w_in": bell_draw(splits[2], (D, FF_WIN), D ** -0.5, 0.078125, ((0, 16), (1, 16))),
        "w_out": bell_draw(splits[3], (FF_WIN, D), FF_WIN ** -0.5, 0.0546875, ((0, 16), (1, 16))),
        "out_grad": bell_draw(splits[4], (TOKENS, D), 0.5, 3.0, ((0, 32), (1, 16))),
    }


def normalize(patches):
    values = patches.astype(jnp.float32)
    average = lax.optimization_barrier(jnp.sum(values, axis=1, keepdims=True)) / D
    squares = lax.optimization_barrier(jnp.sum(values * values, axis=1, keepdims=True)) / D
    inverse = lax.rsqrt(squares - average * average + 1e-06)
    return ((values - average) * inverse, inverse)

def blocked_product(left, right, blocks):
    width = left.shape[1] // blocks

    def step(total, index):
        part_left = lax.dynamic_slice_in_dim(left, index * width, width, 1)
        part_right = lax.dynamic_slice_in_dim(right, index * width, width, 0)
        term = jnp.dot(part_left, part_right, preferred_element_type=jnp.float32).astype(jnp.bfloat16)
        term = lax.optimization_barrier(term)
        return (total + term.astype(jnp.float32), None)
    start_total = jnp.zeros((left.shape[0], right.shape[1]), jnp.float32)
    total, _ = lax.scan(step, start_total, jnp.arange(blocks, dtype=jnp.int32))
    return total

def contract_tokens(left, right):
    return lax.dot_general(left, right, (((0,), (0,)), ((), ())), preferred_element_type=jnp.float32)

def replica_grads(left, right):
    total = jnp.zeros((left.shape[1], right.shape[1]), jnp.float32)
    for group in range(N_DP):
        term = contract_tokens(left[group * TOK_REP:(group + 1) * TOK_REP], right[group * TOK_REP:(group + 1) * TOK_REP])
        term = lax.optimization_barrier(term.astype(jnp.bfloat16))
        total = total + term.astype(jnp.float32)
    return total

def reference(patches, norm_gain, w_in, w_out, out_grad):
    centred, inverse = normalize(patches)
    normed = (centred * norm_gain).astype(jnp.bfloat16)
    pre = blocked_product(normed, w_in, N_ROW)
    activation, slope = jax.vjp(jax.nn.gelu, pre)
    hidden = activation.astype(jnp.bfloat16)
    branch = blocked_product(hidden, w_out, N_COL).astype(jnp.bfloat16)
    hid_grad = blocked_product(out_grad, w_out.T, N_ROW)
    pre_grad = slope(hid_grad)[0].astype(jnp.bfloat16)
    normed_grad = blocked_product(pre_grad, w_in.T, N_COL)
    grad_w_in = replica_grads(normed, pre_grad)
    grad_w_out = replica_grads(hidden, out_grad)
    grad_gain = lax.optimization_barrier(jnp.sum(normed_grad * centred, axis=0))
    scaled = normed_grad * norm_gain
    first = lax.optimization_barrier(jnp.sum(scaled, axis=1, keepdims=True)) / D
    second = lax.optimization_barrier(jnp.sum(scaled * centred, axis=1, keepdims=True)) / D
    grad_patches = (inverse * (scaled - first - centred * second)).astype(jnp.bfloat16)
    return (branch, grad_patches, grad_w_in, grad_w_out, grad_gain)
```

```python
import jax
import jax.numpy as jnp
from jax import lax
from jax.sharding import Mesh, PartitionSpec as P

Y, ZH, X, ZL = 8, 2, 4, 4
ROW = ("y", "zh")
COL = ("x", "zl")
F32, BF16 = jnp.float32, jnp.bfloat16
LANES = 128


def contract_tokens(left, right):
    return lax.dot_general(
        left, right, (((0,), (0,)), ((), ())), preferred_element_type=F32
    )


def contract_last(left, right):
    return lax.dot_general(
        left, right, (((1,), (1,)), ((), ())), preferred_element_type=F32
    )


def shift(values, axis, size, by):
    return lax.ppermute(values, axis, [(i, (i + by) % size) for i in range(size)])


def add(*terms):
    total = terms[0].astype(F32)
    for term in terms[1:]:
        total = total + term.astype(F32)
    return total


def split_high_low(values):
    high = lax.reduce_precision(values, 8, 7)
    return high.astype(BF16), (values - high).astype(BF16)


def as_rows(values, width):
    row = jnp.concatenate(split_high_low(values))
    row = jnp.pad(row, (0, width - row.shape[0]))
    return jnp.broadcast_to(row[None], (8, width))


def whole(rows):
    size = rows.shape[1] // LANES // 2 * LANES
    return rows[0, :size].astype(F32) + rows[0, size : 2 * size].astype(F32)


def gather_x(block):
    half = block.shape[0] // 2
    below, above = shift(block, "x", X, 1), shift(block, "x", X, -1)
    far = (shift(below[:half], "x", X, 1), shift(above[half:], "x", X, -1))
    return block, below, above, jnp.concatenate(far, axis=0)


def scatter_x(own, below, above, far, gain):
    half = own.shape[0] // 2
    up = shift(jnp.concatenate([far[:half], gain], axis=0), "x", X, 1)
    down = shift(jnp.concatenate([far[half:], gain], axis=0), "x", X, -1)
    up_gain, down_gain = up[half:], down[half:]
    up = jnp.concatenate(
        [add(up[:half], above[:half]).astype(BF16), above[half:], up_gain], axis=0
    )
    down = jnp.concatenate(
        [below[:half], add(down[:half], below[half:]).astype(BF16)], axis=0
    )
    up, down = shift(up, "x", X, 1), shift(down, "x", X, -1)
    gains = [whole(g) for g in (gain, up[2 * half :], up_gain, down_gain)]
    gain = (gains[0] + gains[1]) + (gains[2] + gains[3])
    return add(own, up[: 2 * half], down).astype(BF16), gain


def scatter_y(part):
    me = lax.axis_index("y")

    def at(by):
        return part((me + (by + Y)) & (Y - 1))

    far = at(Y // 2)
    half = far.shape[0] // 2
    up, down = shift(far[:half], "y", Y, 1), shift(far[half:], "y", Y, -1)
    above, below = at(Y // 2 - 1), at(1 - Y // 2)
    up = jnp.concatenate([add(up, above[:half]).astype(BF16), above[half:]], axis=0)
    down = jnp.concatenate([below[:half], add(down, below[half:]).astype(BF16)], axis=0)
    for by in range(Y // 2 - 2, -1, -1):
        up, down = shift(up, "y", Y, 1), shift(down, "y", Y, -1)
        if by:
            up, down = add(up, at(by)).astype(BF16), add(down, at(-by)).astype(BF16)
    return add(at(0), up, down)


def gather_y(blocks):
    me, rows = lax.axis_index("y"), blocks[0].shape[0]
    half = rows // 2
    panels = [jnp.zeros((Y * rows, b.shape[1]), b.dtype) for b in blocks]
    edges = [0]
    for b in blocks:
        edges.append(edges[-1] + b.shape[1])

    def put(panels, values, by, offset=0):
        start = ((me + (by + Y)) & (Y - 1)) * rows + offset
        return [
            lax.dynamic_update_slice(
                panel, values[:, low:high], (start, 0), allow_negative_indices=False
            )
            for panel, low, high in zip(panels, edges[:-1], edges[1:])
        ]

    block = jnp.concatenate(blocks, axis=1)
    panels = put(panels, block, 0)
    below = above = block
    for by in range(1, Y // 2):
        below, above = shift(below, "y", Y, 1), shift(above, "y", Y, -1)
        panels = put(put(panels, below, -by), above, by)
    panels = put(panels, shift(below[:half], "y", Y, 1), Y // 2)
    return put(panels, shift(above[half:], "y", Y, -1), Y // 2, half)


def shards(patches, norm_gain, w_in, w_out, out_grad):
    tokens, width = patches.shape
    hidden_width = w_in.shape[1]
    model_width = width * Y * ZH
    values = patches.astype(F32)
    image = jnp.sum(norm_gain[:, None] * w_in.astype(F32), axis=0)
    mine = jnp.concatenate([jnp.sum(values, axis=1), jnp.sum(values * values, axis=1), image])
    theirs = lax.all_to_all(
        jnp.broadcast_to(mine, (Y * ZH,) + mine.shape), ROW, 0, 0, tiled=True
    )
    sums = jnp.sum(theirs, axis=0)
    average = (sums[:tokens] / model_width)[:, None]
    squares = (sums[tokens : 2 * tokens] / model_width)[:, None]
    image = sums[2 * tokens :]
    inverse = lax.rsqrt(squares - average * average + 1e-06)
    centred = (values - average) * inverse
    normed = (centred * norm_gain).astype(BF16)
    both = lax.all_gather(
        jnp.concatenate([normed, out_grad], axis=1), "zl", axis=0, tiled=True
    )
    both = jnp.concatenate(gather_x(both), axis=0)
    normed_panel, cotangent = both[:, :width], both[:, width:]
    pre_part = jnp.dot(normed_panel, w_in, preferred_element_type=F32).astype(BF16)
    hid_part = contract_last(cotangent, w_out).astype(BF16)
    rows = both.shape[0] // Y

    def part(place):
        return jnp.concatenate(
            [
                lax.dynamic_slice(
                    a, (place * rows, 0), (rows, hidden_width), allow_negative_indices=False
                )
                for a in (pre_part, hid_part)
            ],
            axis=1,
        )

    half_sum = scatter_y(part).astype(BF16)
    total = add(half_sum, shift(half_sum, "zh", ZH, 1))
    pre, hid_grad = total[:, :hidden_width], total[:, hidden_width:]
    activation, slope = jax.vjp(jax.nn.gelu, pre)
    pre_grad = slope(hid_grad)[0].astype(BF16)
    first = jnp.sum(pre_grad.astype(F32) * image, axis=1, keepdims=True)
    second = jnp.sum(pre_grad.astype(F32) * pre, axis=1, keepdims=True)
    lane = lax.broadcasted_iota(jnp.int32, (rows, LANES), 1)
    shares = jnp.zeros((rows, LANES), BF16)
    for place, term in enumerate(split_high_low(first) + split_high_low(second)):
        shares = jnp.where(lane == place, term, shares)
    hidden_panel, pre_grad_panel, shares = gather_y(
        [activation.astype(BF16), pre_grad, shares]
    )
    branch_part = jnp.dot(hidden_panel, w_out, preferred_element_type=F32).astype(BF16)
    normed_grad_part = contract_last(pre_grad_panel, w_in)
    gain_part = jnp.sum(normed_grad_part * normed_panel.astype(F32), axis=0)
    sent = jnp.concatenate([branch_part, normed_grad_part.astype(BF16), shares], axis=1)
    block = both.shape[0] // X
    parts = [sent[i * block : (i + 1) * block] for i in range(X)]
    back, gain_part = scatter_x(*parts, as_rows(gain_part, sent.shape[1]))
    back = back.reshape(ZL, tokens, -1)
    gain_part = jnp.broadcast_to(as_rows(gain_part, sent.shape[1])[None], (ZL, 8, sent.shape[1]))
    back = lax.all_to_all(
        jnp.concatenate([back, gain_part], axis=1), "zl", 0, 0, tiled=True
    )
    gain_sum = whole(jnp.sum(back[:, tokens : tokens + 1].astype(F32), axis=0))
    back = jnp.sum(back[:, :tokens].astype(F32), axis=0)
    branch = back[:, :width].astype(BF16)
    normed_grad = back[:, width : 2 * width]
    rest = back[:, 2 * width :]
    lane = lax.broadcasted_iota(jnp.int32, rest.shape, 1)
    first = jnp.sum(jnp.where(lane < 2, rest, 0), axis=1, keepdims=True) / model_width
    second = jnp.sum(jnp.where(lane >= 2, rest, 0), axis=1, keepdims=True) / model_width
    grad_gain = (gain_sum + shift(gain_sum, "dp", 2, 1)) / norm_gain
    grad_patches = inverse * (normed_grad * norm_gain - first - centred * second)
    local_in = contract_tokens(normed_panel, pre_grad_panel).astype(BF16)
    local_out = contract_tokens(hidden_panel, cotangent).astype(BF16)
    grad_w_in = add(local_in, shift(local_in, "dp", 2, 1))
    grad_w_out = add(local_out, shift(local_out, "dp", 2, 1))
    return (branch, grad_patches.astype(BF16), grad_w_in, grad_w_out, grad_gain)


def solution(mesh):
    fine = Mesh(mesh.devices.reshape(-1, Y, ZH, X, ZL), ("dp",) + ROW + COL)
    return jax.shard_map(
        shards,
        mesh=fine,
        in_specs=(
            P(("dp",) + COL, ROW),
            P(ROW),
            P(ROW, COL),
            P(COL, ROW),
            P(("dp",) + COL, ROW),
        ),
        out_specs=(
            P(("dp",) + COL, ROW),
            P(("dp",) + COL, ROW),
            P(ROW, COL),
            P(COL, ROW),
            P(ROW),
        ),
        check_vma=False,
    )
```

```python
import jax
import jax.numpy as jnp
from jax import lax
from jax.sharding import Mesh, PartitionSpec as P

Y, ZH, X, ZL = 8, 2, 4, 4
ROW = ("y", "zh")
COL = ("x", "zl")
F32, BF16 = jnp.float32, jnp.bfloat16
LANES = 128


def contract_tokens(left, right):
    return lax.dot_general(
        left, right, (((0,), (0,)), ((), ())), preferred_element_type=F32
    )


def contract_last(left, right):
    return lax.dot_general(
        left, right, (((1,), (1,)), ((), ())), preferred_element_type=F32
    )


def shift(values, axis, size, by):
    return lax.ppermute(values, axis, [(i, (i + by) % size) for i in range(size)])


def add(*terms):
    total = terms[0].astype(F32)
    for term in terms[1:]:
        total = total + term.astype(F32)
    return total


def to_all(values, axes):
    count = {ROW: Y * ZH, COL: X * ZL}[axes]
    copies = jnp.broadcast_to(values, (count,) + values.shape)
    return lax.all_to_all(copies, axes, 0, 0, tiled=True)


def split_high_low(values):
    high = lax.reduce_precision(values, 8, 7)
    return high.astype(BF16), (values - high).astype(BF16)


def scatter_y(part):
    me = lax.axis_index("y")

    def at(by):
        return part((me + (by + Y)) & (Y - 1))

    far = at(Y // 2)
    half = far.shape[0] // 2
    up, down = shift(far[:half], "y", Y, 1), shift(far[half:], "y", Y, -1)
    above, below = at(Y // 2 - 1), at(1 - Y // 2)
    up = jnp.concatenate([add(up, above[:half]).astype(BF16), above[half:]], axis=0)
    down = jnp.concatenate([below[:half], add(down, below[half:]).astype(BF16)], axis=0)
    for by in range(Y // 2 - 2, -1, -1):
        up, down = shift(up, "y", Y, 1), shift(down, "y", Y, -1)
        if by:
            up, down = add(up, at(by)).astype(BF16), add(down, at(-by)).astype(BF16)
    return add(at(0), up, down)


def gather_ring(blocks, axis, size):
    me, rows = lax.axis_index(axis), blocks[0].shape[0]
    half = rows // 2
    panels = [jnp.zeros((size * rows, b.shape[1]), b.dtype) for b in blocks]
    edges = [0]
    for b in blocks:
        edges.append(edges[-1] + b.shape[1])

    def put(panels, values, by, offset=0):
        start = ((me + (by + size)) & (size - 1)) * rows + offset
        return [
            lax.dynamic_update_slice(
                panel, values[:, low:high], (start, 0), allow_negative_indices=False
            )
            for panel, low, high in zip(panels, edges[:-1], edges[1:])
        ]

    block = jnp.concatenate(blocks, axis=1)
    panels = put(panels, block, 0)
    below = above = block
    for by in range(1, size // 2):
        below, above = shift(below, axis, size, 1), shift(above, axis, size, -1)
        panels = put(put(panels, below, -by), above, by)
    panels = put(panels, shift(below[:half], axis, size, 1), size // 2)
    return put(panels, shift(above[half:], axis, size, -1), size // 2, half)


def scatter(sent, vector, axis, size):
    width, long = sent.shape[1], vector.shape[0]
    row = jnp.pad(jnp.concatenate(split_high_low(vector)), (0, width - 2 * long))
    parts = jnp.concatenate(
        [sent.reshape(size, -1, width), jnp.broadcast_to(row, (size, 8, width))], axis=1
    )
    back = lax.all_to_all(parts, axis, 0, 0, tiled=True)
    rows = back.shape[1] - 8
    row = jnp.sum(back[:, rows].astype(F32), axis=0)
    total = jnp.sum(back[:, :rows].astype(F32), axis=0)
    return total, row[:long] + row[long : 2 * long]


def shards(patches, norm_gain, w_in, w_out, out_grad):
    tokens, width = patches.shape
    hidden_width = w_in.shape[1]
    model_width = width * Y * ZH
    both = lax.all_gather(
        jnp.concatenate([patches, out_grad], axis=1), "zl", axis=0, tiled=True
    )
    both = gather_ring([both], "x", X)[0]
    values = patches.astype(F32)
    image = jnp.sum(norm_gain[:, None] * w_in.astype(F32), axis=0)
    sums = jnp.sum(
        to_all(
            jnp.concatenate([jnp.sum(values, axis=1), jnp.sum(values * values, axis=1), image]),
            ROW,
        ),
        axis=0,
    )
    average = sums[:tokens] / model_width
    squares = sums[tokens : 2 * tokens] / model_width
    image = sums[2 * tokens :]
    inverse = lax.rsqrt(squares - average * average + 1e-06)
    scales = to_all(jnp.concatenate([average, inverse]), COL)
    averages = scales[:, :tokens].reshape(-1, 1)
    inverses = scales[:, tokens:].reshape(-1, 1)
    average, inverse = average[:, None], inverse[:, None]
    centred = (values - average) * inverse
    normed_panel = both[:, :width].astype(F32)
    normed_panel = ((normed_panel - averages) * inverses * norm_gain).astype(BF16)
    cotangent = both[:, width:]
    pre_part = jnp.dot(normed_panel, w_in, preferred_element_type=F32).astype(BF16)
    hid_part = contract_last(cotangent, w_out).astype(BF16)
    rows = both.shape[0] // Y

    def part(place):
        return jnp.concatenate(
            [
                lax.dynamic_slice(
                    a, (place * rows, 0), (rows, hidden_width), allow_negative_indices=False
                )
                for a in (pre_part, hid_part)
            ],
            axis=1,
        )

    half_sum = scatter_y(part).astype(BF16)
    total = add(half_sum, shift(half_sum, "zh", ZH, 1))
    pre, hid_grad = total[:, :hidden_width], total[:, hidden_width:]
    activation, slope = jax.vjp(jax.nn.gelu, pre)
    pre_grad = slope(hid_grad)[0].astype(BF16)
    first = jnp.sum(pre_grad.astype(F32) * image, axis=1, keepdims=True)
    second = jnp.sum(pre_grad.astype(F32) * pre, axis=1, keepdims=True)
    lane = lax.broadcasted_iota(jnp.int32, (rows, LANES), 1)
    shares = jnp.zeros((rows, LANES), BF16)
    for place, term in enumerate(split_high_low(first) + split_high_low(second)):
        shares = jnp.where(lane == place, term, shares)
    hidden_panel, pre_grad_panel, shares = gather_ring(
        [activation.astype(BF16), pre_grad, shares], "y", Y
    )
    branch_part = jnp.dot(hidden_panel, w_out, preferred_element_type=F32).astype(BF16)
    normed_grad_part = contract_last(pre_grad_panel, w_in)
    gain_part = jnp.sum(normed_grad_part * normed_panel.astype(F32), axis=0)
    sent = jnp.concatenate([branch_part, normed_grad_part.astype(BF16), shares], axis=1)
    back, gain_sum = scatter(sent, gain_part, "x", X)
    back, gain_sum = scatter(back.astype(BF16), gain_sum, "zl", ZL)
    branch = back[:, :width].astype(BF16)
    normed_grad = back[:, width : 2 * width]
    rest = back[:, 2 * width :]
    lane = lax.broadcasted_iota(jnp.int32, rest.shape, 1)
    first = jnp.sum(jnp.where(lane < 2, rest, 0), axis=1, keepdims=True) / model_width
    second = jnp.sum(jnp.where(lane >= 2, rest, 0), axis=1, keepdims=True) / model_width
    grad_gain = (gain_sum + shift(gain_sum, "dp", 2, 1)) / norm_gain
    grad_patches = inverse * (normed_grad * norm_gain - first - centred * second)
    local_in = contract_tokens(normed_panel, pre_grad_panel).astype(BF16)
    local_out = contract_tokens(hidden_panel, cotangent).astype(BF16)
    grad_w_in = add(local_in, shift(local_in, "dp", 2, 1))
    grad_w_out = add(local_out, shift(local_out, "dp", 2, 1))
    return (branch, grad_patches.astype(BF16), grad_w_in, grad_w_out, grad_gain)


def solution(mesh):
    fine = Mesh(mesh.devices.reshape(-1, Y, ZH, X, ZL), ("dp",) + ROW + COL)
    return jax.shard_map(
        shards,
        mesh=fine,
        in_specs=(
            P(("dp",) + COL, ROW),
            P(ROW),
            P(ROW, COL),
            P(COL, ROW),
            P(("dp",) + COL, ROW),
        ),
        out_specs=(
            P(("dp",) + COL, ROW),
            P(("dp",) + COL, ROW),
            P(ROW, COL),
            P(COL, ROW),
            P(ROW),
        ),
        check_vma=False,
    )
```

```python
import jax
import jax.numpy as jnp
from jax import lax
from jax.experimental.layout import Layout, with_layout_constraint
from jax.sharding import Mesh, PartitionSpec as P

Y, ZH, X, ZL = 8, 2, 4, 4
ROW = ("y", "zh")
COL = ("x", "zl")
F32, BF16 = jnp.float32, jnp.bfloat16
LANES = 128


def contract_tokens(left, right):
    return lax.dot_general(
        left, right, (((0,), (0,)), ((), ())), preferred_element_type=F32
    )


def contract_last(left, right):
    return lax.dot_general(
        left, right, (((1,), (1,)), ((), ())), preferred_element_type=F32
    )


def shift(values, axis, size, by):
    return lax.ppermute(values, axis, [(i, (i + by) % size) for i in range(size)])


def row_major(values):
    return with_layout_constraint(values, Layout((0, 1)))


def add(*terms):
    total = terms[0].astype(F32)
    for term in terms[1:]:
        total = total + term.astype(F32)
    return total


def to_all(values, axes):
    count = {ROW: Y * ZH, COL: X * ZL}[axes]
    copies = jnp.broadcast_to(values, (count,) + values.shape)
    return lax.all_to_all(copies, axes, 0, 0, tiled=True)


def split_high_low(values):
    high = lax.reduce_precision(values, 8, 7)
    return high.astype(BF16), (values - high).astype(BF16)


def scatter_y(part):
    me = lax.axis_index("y")

    def at(by):
        return part((me + (by + Y)) & (Y - 1))

    far = at(Y // 2)
    half = far.shape[0] // 2
    up, down = shift(far[:half], "y", Y, 1), shift(far[half:], "y", Y, -1)
    above, below = at(Y // 2 - 1), at(1 - Y // 2)
    up = jnp.concatenate([add(up, above[:half]).astype(BF16), above[half:]], axis=0)
    down = jnp.concatenate([below[:half], add(down, below[half:]).astype(BF16)], axis=0)
    for by in range(Y // 2 - 2, -1, -1):
        up, down = shift(up, "y", Y, 1), shift(down, "y", Y, -1)
        if by:
            up, down = add(up, at(by)).astype(BF16), add(down, at(-by)).astype(BF16)
    return add(at(0), up, down)


def gather_ring(blocks, axis, size):
    me, rows = lax.axis_index(axis), blocks[0].shape[0]
    half = rows // 2
    panels = [jnp.zeros((size * rows, b.shape[1]), b.dtype) for b in blocks]
    edges = [0]
    for b in blocks:
        edges.append(edges[-1] + b.shape[1])

    def put(panels, values, by, offset=0):
        start = ((me + (by + size)) & (size - 1)) * rows + offset
        return [
            lax.dynamic_update_slice(
                panel, values[:, low:high], (start, 0), allow_negative_indices=False
            )
            for panel, low, high in zip(panels, edges[:-1], edges[1:])
        ]

    block = jnp.concatenate(blocks, axis=1)
    panels = put(panels, block, 0)
    below = above = block
    for by in range(1, size // 2):
        below, above = shift(below, axis, size, 1), shift(above, axis, size, -1)
        panels = put(put(panels, below, -by), above, by)
    panels = put(panels, shift(below[:half], axis, size, 1), size // 2)
    return put(panels, shift(above[half:], axis, size, -1), size // 2, half)


def scatter(sent, vector, axis, size):
    width, long = sent.shape[1], vector.shape[0]
    row = jnp.pad(jnp.concatenate(split_high_low(vector)), (0, width - 2 * long))
    parts = jnp.concatenate(
        [sent.reshape(size, -1, width), jnp.broadcast_to(row, (size, 8, width))], axis=1
    )
    back = lax.all_to_all(parts, axis, 0, 0, tiled=True)
    rows = back.shape[1] - 8
    row = jnp.sum(back[:, rows].astype(F32), axis=0)
    total = jnp.sum(back[:, :rows].astype(F32), axis=0)
    return total, row[:long] + row[long : 2 * long]


def shards(patches, norm_gain, w_in, w_out, out_grad):
    tokens, width = patches.shape
    hidden_width = w_in.shape[1]
    model_width = width * Y * ZH
    near = lax.all_gather(
        jnp.concatenate([patches, out_grad], axis=1), "zl", axis=0, tiled=True
    )
    cotangent = near[:, width:]
    below, above = shift(cotangent, "x", X, 1), shift(cotangent, "x", X, -1)
    values = near[:, :width].astype(F32)
    image = jnp.sum(norm_gain[:, None] * w_in.astype(F32), axis=0)
    sums = jnp.sum(
        to_all(
            jnp.concatenate([jnp.sum(values, axis=1), jnp.sum(values * values, axis=1), image]),
            ROW,
        ),
        axis=0,
    )
    count = near.shape[0]
    average = (sums[:count] / model_width)[:, None]
    squares = (sums[count : 2 * count] / model_width)[:, None]
    image = sums[2 * count :]
    inverse = lax.rsqrt(squares - average * average + 1e-06)
    centred = (values - average) * inverse
    normed, below, above = lax.optimization_barrier(
        ((centred * norm_gain).astype(BF16), below, above)
    )
    half = count // 2
    place = lax.axis_index("x")

    def panel(own, below, above, far):
        whole = jnp.zeros((X * count, width), BF16)
        for by, block in ((0, own), (-1, below), (1, above), (2, far)):
            start = ((place + (by + X)) & (X - 1)) * count
            whole = lax.dynamic_update_slice(
                whole, block, (start, 0), allow_negative_indices=False
            )
        return whole

    up = shift(jnp.concatenate([normed, below[:half]], axis=0), "x", X, 1)
    down = shift(jnp.concatenate([normed, above[half:]], axis=0), "x", X, -1)
    far = jnp.concatenate([up[count:], down[count:]], axis=0)
    cotangent = panel(cotangent, below, above, far)
    below, above = up[:count], down[:count]
    far = shift(below[:half], "x", X, 1), shift(above[half:], "x", X, -1)
    normed_panel = panel(normed, below, above, jnp.concatenate(far, axis=0))
    own = lax.axis_index("zl") * tokens
    centred, inverse = (
        lax.dynamic_slice(
            a, (own, 0), (tokens, a.shape[1]), allow_negative_indices=False
        )
        for a in (centred, inverse)
    )
    pre_part = jnp.dot(normed_panel, w_in, preferred_element_type=F32).astype(BF16)
    hid_part = contract_last(cotangent, w_out).astype(BF16)
    rows = cotangent.shape[0] // Y

    def part(place):
        return jnp.concatenate(
            [
                lax.dynamic_slice(
                    a, (place * rows, 0), (rows, hidden_width), allow_negative_indices=False
                )
                for a in (pre_part, hid_part)
            ],
            axis=1,
        )

    half_sum = scatter_y(part).astype(BF16)
    total = add(half_sum, shift(half_sum, "zh", ZH, 1))
    pre, hid_grad = total[:, :hidden_width], total[:, hidden_width:]
    activation, slope = jax.vjp(jax.nn.gelu, pre)
    pre_grad = slope(hid_grad)[0].astype(BF16)
    first = jnp.sum(pre_grad.astype(F32) * image, axis=1, keepdims=True)
    second = jnp.sum(pre_grad.astype(F32) * pre, axis=1, keepdims=True)
    lane = lax.broadcasted_iota(jnp.int32, (rows, LANES), 1)
    shares = jnp.zeros((rows, LANES), BF16)
    for place, term in enumerate(split_high_low(first) + split_high_low(second)):
        shares = jnp.where(lane == place, term, shares)
    hidden_panel, pre_grad_panel, shares = gather_ring(
        [activation.astype(BF16), pre_grad, shares], "y", Y
    )
    branch_part = jnp.dot(hidden_panel, w_out, preferred_element_type=F32).astype(BF16)
    normed_grad_part = contract_last(pre_grad_panel, w_in)
    gain_part = jnp.sum(normed_grad_part * normed_panel.astype(F32), axis=0)
    sent = row_major(
        jnp.concatenate([branch_part, normed_grad_part.astype(BF16), shares], axis=1)
    )
    back, gain_sum = scatter(sent, gain_part, "x", X)
    back, gain_sum = scatter(back.astype(BF16), gain_sum, "zl", ZL)
    branch = back[:, :width].astype(BF16)
    normed_grad = back[:, width : 2 * width]
    rest = back[:, 2 * width :]
    lane = lax.broadcasted_iota(jnp.int32, rest.shape, 1)
    first = jnp.sum(jnp.where(lane < 2, rest, 0), axis=1, keepdims=True) / model_width
    second = jnp.sum(jnp.where(lane >= 2, rest, 0), axis=1, keepdims=True) / model_width
    grad_gain = (gain_sum + shift(gain_sum, "dp", 2, 1)) / norm_gain
    grad_patches = inverse * (normed_grad * norm_gain - first - centred * second)
    local_in = contract_tokens(normed_panel, pre_grad_panel).astype(BF16)
    local_out = contract_tokens(hidden_panel, cotangent).astype(BF16)
    grad_w_in = add(local_in, shift(local_in, "dp", 2, 1))
    grad_w_out = add(local_out, shift(local_out, "dp", 2, 1))
    return (branch, grad_patches.astype(BF16), grad_w_in, grad_w_out, grad_gain)


def solution(mesh):
    fine = Mesh(mesh.devices.reshape(-1, Y, ZH, X, ZL), ("dp",) + ROW + COL)
    return jax.shard_map(
        shards,
        mesh=fine,
        in_specs=(
            P(("dp",) + COL, ROW),
            P(ROW),
            P(ROW, COL),
            P(COL, ROW),
            P(("dp",) + COL, ROW),
        ),
        out_specs=(
            P(("dp",) + COL, ROW),
            P(("dp",) + COL, ROW),
            P(ROW, COL),
            P(COL, ROW),
            P(ROW),
        ),
        check_vma=False,
    )
```

```python
import jax
import jax.numpy as jnp
from jax import lax
from jax.experimental.layout import Layout, with_layout_constraint
from jax.sharding import Mesh, PartitionSpec as P

Y, ZH, X, ZL = 8, 2, 4, 4
ROW = ("y", "zh")
COL = ("x", "zl")
F32, BF16 = jnp.float32, jnp.bfloat16
LANES = 128


def contract_tokens(left, right):
    return lax.dot_general(
        left, right, (((0,), (0,)), ((), ())), preferred_element_type=F32
    )


def contract_last(left, right):
    return lax.dot_general(
        left, right, (((1,), (1,)), ((), ())), preferred_element_type=F32
    )


def swap(values, axis):
    return lax.ppermute(values, axis, [(0, 1), (1, 0)])


def shift(values, axis, size, by):
    pairs = [(i, (i + by) % size) for i in range(size)]
    pairs += [(size + i, size + (i - by) % size) for i in range(size)]
    return lax.ppermute(values, ("dp", axis), pairs)


def places(axis, size):
    me, way = lax.axis_index(axis) + size, 1 - 2 * lax.axis_index("dp")
    return lambda by: (me + by * way) & (size - 1)


def row_major(values):
    return with_layout_constraint(values, Layout((0, 1)))


def add(*terms):
    total = terms[0].astype(F32)
    for term in terms[1:]:
        total = total + term.astype(F32)
    return total


def to_all(values, axes):
    count = {ROW: Y * ZH, COL: X * ZL}[axes]
    copies = jnp.broadcast_to(values, (count,) + values.shape)
    return lax.all_to_all(copies, axes, 0, 0, tiled=True)


def split_high_low(values):
    high = lax.reduce_precision(values, 8, 7)
    return high.astype(BF16), (values - high).astype(BF16)


def scatter_y(part):
    place = places("y", Y)

    def at(by):
        return part(place(by))

    far = at(Y // 2)
    half = far.shape[0] // 2
    up, down = shift(far[:half], "y", Y, 1), shift(far[half:], "y", Y, -1)
    above, below = at(Y // 2 - 1), at(1 - Y // 2)
    up = jnp.concatenate([add(up, above[:half]).astype(BF16), above[half:]], axis=0)
    down = jnp.concatenate([below[:half], add(down, below[half:]).astype(BF16)], axis=0)
    for by in range(Y // 2 - 2, -1, -1):
        up, down = shift(up, "y", Y, 1), shift(down, "y", Y, -1)
        if by:
            up, down = add(up, at(by)).astype(BF16), add(down, at(-by)).astype(BF16)
    return add(at(0), up, down)


def gather_ring(blocks, axis, size):
    place, rows = places(axis, size), blocks[0].shape[0]
    half = rows // 2
    panels = [jnp.zeros((size * rows, b.shape[1]), b.dtype) for b in blocks]
    edges = [0]
    for b in blocks:
        edges.append(edges[-1] + b.shape[1])

    def put(panels, values, by, offset=0):
        start = place(by) * rows + offset
        return [
            lax.dynamic_update_slice(
                panel, values[:, low:high], (start, 0), allow_negative_indices=False
            )
            for panel, low, high in zip(panels, edges[:-1], edges[1:])
        ]

    block = jnp.concatenate(blocks, axis=1)
    panels = put(panels, block, 0)
    below = above = block
    for by in range(1, size // 2):
        below, above = shift(below, axis, size, 1), shift(above, axis, size, -1)
        panels = put(put(panels, below, -by), above, by)
    panels = put(panels, shift(below[:half], axis, size, 1), size // 2)
    return put(panels, shift(above[half:], axis, size, -1), size // 2, half)


def scatter(sent, vector, axis, size):
    width, long = sent.shape[1], vector.shape[0]
    row = jnp.pad(jnp.concatenate(split_high_low(vector)), (0, width - 2 * long))
    parts = jnp.concatenate(
        [sent.reshape(size, -1, width), jnp.broadcast_to(row, (size, 8, width))], axis=1
    )
    back = lax.all_to_all(parts, axis, 0, 0, tiled=True)
    rows = back.shape[1] - 8
    row = jnp.sum(back[:, rows].astype(F32), axis=0)
    total = jnp.sum(back[:, :rows].astype(F32), axis=0)
    return total, row[:long] + row[long : 2 * long]


def shards(patches, norm_gain, w_in, w_out, out_grad):
    tokens, width = patches.shape
    hidden_width = w_in.shape[1]
    model_width = width * Y * ZH
    near = lax.all_gather(
        jnp.concatenate([patches, out_grad], axis=1), "zl", axis=0, tiled=True
    )
    cotangent = near[:, width:]
    below, above = shift(cotangent, "x", X, 1), shift(cotangent, "x", X, -1)
    values = near[:, :width].astype(F32)
    image = jnp.sum(norm_gain[:, None] * w_in.astype(F32), axis=0)
    sums = jnp.sum(
        to_all(
            jnp.concatenate([jnp.sum(values, axis=1), jnp.sum(values * values, axis=1), image]),
            ROW,
        ),
        axis=0,
    )
    count = near.shape[0]
    average = (sums[:count] / model_width)[:, None]
    squares = (sums[count : 2 * count] / model_width)[:, None]
    image = sums[2 * count :]
    inverse = lax.rsqrt(squares - average * average + 1e-06)
    centred = (values - average) * inverse
    normed, below, above = lax.optimization_barrier(
        ((centred * norm_gain).astype(BF16), below, above)
    )
    half = count // 2
    place = places("x", X)

    def panel(own, below, above, far):
        whole = jnp.zeros((X * count, width), BF16)
        for by, block in ((0, own), (-1, below), (1, above), (2, far)):
            whole = lax.dynamic_update_slice(
                whole, block, (place(by) * count, 0), allow_negative_indices=False
            )
        return whole

    up = shift(jnp.concatenate([normed, below[:half]], axis=0), "x", X, 1)
    down = shift(jnp.concatenate([normed, above[half:]], axis=0), "x", X, -1)
    far = jnp.concatenate([up[count:], down[count:]], axis=0)
    cotangent = panel(cotangent, below, above, far)
    below, above = up[:count], down[:count]
    far = shift(below[:half], "x", X, 1), shift(above[half:], "x", X, -1)
    normed_panel = panel(normed, below, above, jnp.concatenate(far, axis=0))
    own = lax.axis_index("zl") * tokens
    centred, inverse = (
        lax.dynamic_slice(
            a, (own, 0), (tokens, a.shape[1]), allow_negative_indices=False
        )
        for a in (centred, inverse)
    )
    pre_part = jnp.dot(normed_panel, w_in, preferred_element_type=F32).astype(BF16)
    hid_part = contract_last(cotangent, w_out).astype(BF16)
    rows = cotangent.shape[0] // Y

    def part(place):
        return jnp.concatenate(
            [
                lax.dynamic_slice(
                    a, (place * rows, 0), (rows, hidden_width), allow_negative_indices=False
                )
                for a in (pre_part, hid_part)
            ],
            axis=1,
        )

    half_sum = scatter_y(part).astype(BF16)
    total = add(half_sum, swap(half_sum, "zh"))
    pre, hid_grad = total[:, :hidden_width], total[:, hidden_width:]
    activation, slope = jax.vjp(jax.nn.gelu, pre)
    pre_grad = slope(hid_grad)[0].astype(BF16)
    first = jnp.sum(pre_grad.astype(F32) * image, axis=1, keepdims=True)
    second = jnp.sum(pre_grad.astype(F32) * pre, axis=1, keepdims=True)
    lane = lax.broadcasted_iota(jnp.int32, (rows, LANES), 1)
    shares = jnp.zeros((rows, LANES), BF16)
    for spot, term in enumerate(split_high_low(first) + split_high_low(second)):
        shares = jnp.where(lane == spot, term, shares)
    hidden_panel, pre_grad_panel, shares = gather_ring(
        [activation.astype(BF16), pre_grad, shares], "y", Y
    )
    branch_part = jnp.dot(hidden_panel, w_out, preferred_element_type=F32).astype(BF16)
    normed_grad_part = contract_last(pre_grad_panel, w_in)
    gain_part = jnp.sum(normed_grad_part * normed_panel.astype(F32), axis=0)
    sent = row_major(
        jnp.concatenate([branch_part, normed_grad_part.astype(BF16), shares], axis=1)
    )
    back, gain_sum = scatter(sent, gain_part, "x", X)
    back, gain_sum = scatter(back.astype(BF16), gain_sum, "zl", ZL)
    branch = back[:, :width].astype(BF16)
    normed_grad = back[:, width : 2 * width]
    rest = back[:, 2 * width :]
    lane = lax.broadcasted_iota(jnp.int32, rest.shape, 1)
    first = jnp.sum(jnp.where(lane < 2, rest, 0), axis=1, keepdims=True) / model_width
    second = jnp.sum(jnp.where(lane >= 2, rest, 0), axis=1, keepdims=True) / model_width
    grad_gain = (gain_sum + swap(gain_sum, "dp")) / norm_gain
    grad_patches = inverse * (normed_grad * norm_gain - first - centred * second)
    local_in = contract_tokens(normed_panel, pre_grad_panel).astype(BF16)
    local_out = contract_tokens(hidden_panel, cotangent).astype(BF16)
    grad_w_in = add(local_in, swap(local_in, "dp"))
    grad_w_out = add(local_out, swap(local_out, "dp"))
    return (branch, grad_patches.astype(BF16), grad_w_in, grad_w_out, grad_gain)


def solution(mesh):
    fine = Mesh(mesh.devices.reshape(-1, Y, ZH, X, ZL), ("dp",) + ROW + COL)
    return jax.shard_map(
        shards,
        mesh=fine,
        in_specs=(
            P(("dp",) + COL, ROW),
            P(ROW),
            P(ROW, COL),
            P(COL, ROW),
            P(("dp",) + COL, ROW),
        ),
        out_specs=(
            P(("dp",) + COL, ROW),
            P(("dp",) + COL, ROW),
            P(ROW, COL),
            P(COL, ROW),
            P(ROW),
        ),
        check_vma=False,
    )
```

```python
import jax
import jax.numpy as jnp
from jax import lax
from jax.experimental.layout import Layout, with_layout_constraint
from jax.sharding import Mesh, PartitionSpec as P

Y, ZH, X, ZL = 8, 2, 4, 4
ROW = ("y", "zh")
COL = ("x", "zl")
F32, BF16 = jnp.float32, jnp.bfloat16
LANES = 128


def contract_tokens(left, right):
    return lax.dot_general(
        left, right, (((0,), (0,)), ((), ())), preferred_element_type=F32
    )


def contract_last(left, right):
    return lax.dot_general(
        left, right, (((1,), (1,)), ((), ())), preferred_element_type=F32
    )


def shift(values, axis, size, by):
    return lax.ppermute(values, axis, [(i, (i + by) % size) for i in range(size)])


def row_major(values):
    return with_layout_constraint(values, Layout((0, 1)))


def add(*terms):
    total = terms[0].astype(F32)
    for term in terms[1:]:
        total = total + term.astype(F32)
    return total


def to_all(values, axes):
    count = {ROW: Y * ZH, COL: X * ZL}[axes]
    copies = jnp.broadcast_to(values, (count,) + values.shape)
    return lax.all_to_all(copies, axes, 0, 0, tiled=True)


def split_high_low(values):
    high = lax.reduce_precision(values, 8, 7)
    return high.astype(BF16), (values - high).astype(BF16)


def scatter_y(part):
    me = lax.axis_index("y")

    def at(by):
        return part((me + (by + Y)) & (Y - 1))

    far = at(4)
    half = far.shape[0] // 2
    up, down = shift(at(3), "y", Y, 1), shift(at(-3), "y", Y, -1)
    up_far, down_far = shift(far[:half], "y", Y, 2), shift(far[half:], "y", Y, -2)
    above, below = at(2), at(-2)
    up = jnp.concatenate(
        [
            add(up[:half], up_far, above[:half]).astype(BF16),
            add(up[half:], above[half:]).astype(BF16),
        ],
        axis=0,
    )
    down = jnp.concatenate(
        [
            add(down[:half], below[:half]).astype(BF16),
            add(down[half:], down_far, below[half:]).astype(BF16),
        ],
        axis=0,
    )
    up, down = shift(up, "y", Y, 1), shift(down, "y", Y, -1)
    up, down = add(up, at(1)).astype(BF16), add(down, at(-1)).astype(BF16)
    up, down = shift(up, "y", Y, 1), shift(down, "y", Y, -1)
    return add(at(0), up, down)


def gather_ring(blocks, axis, size):
    me, rows = lax.axis_index(axis), blocks[0].shape[0]
    half = rows // 2
    panels = [jnp.zeros((size * rows, b.shape[1]), b.dtype) for b in blocks]
    edges = [0]
    for b in blocks:
        edges.append(edges[-1] + b.shape[1])

    def put(panels, values, by, offset=0):
        start = ((me + (by + size)) & (size - 1)) * rows + offset
        return [
            lax.dynamic_update_slice(
                panel, values[:, low:high], (start, 0), allow_negative_indices=False
            )
            for panel, low, high in zip(panels, edges[:-1], edges[1:])
        ]

    block = jnp.concatenate(blocks, axis=1)
    panels = put(panels, block, 0)
    below = above = block
    for by in range(1, size // 2 - 1):
        below, above = shift(below, axis, size, 1), shift(above, axis, size, -1)
        panels = put(put(panels, below, -by), above, by)
    by = size // 2
    low = shift(below, axis, size, 1), shift(below[:half], axis, size, 2)
    high = shift(above, axis, size, -1), shift(above[half:], axis, size, -2)
    panels = put(put(panels, low[0], 1 - by), high[0], by - 1)
    return put(put(panels, low[1], by), high[1], by, half)


def scatter(sent, vector, axis, size):
    width, long = sent.shape[1], vector.shape[0]
    row = jnp.pad(jnp.concatenate(split_high_low(vector)), (0, width - 2 * long))
    parts = jnp.concatenate(
        [sent.reshape(size, -1, width), jnp.broadcast_to(row, (size, 8, width))], axis=1
    )
    back = lax.all_to_all(parts, axis, 0, 0, tiled=True)
    rows = back.shape[1] - 8
    row = jnp.sum(back[:, rows].astype(F32), axis=0)
    total = jnp.sum(back[:, :rows].astype(F32), axis=0)
    return total, row[:long] + row[long : 2 * long]


def shards(patches, norm_gain, w_in, w_out, out_grad):
    tokens, width = patches.shape
    hidden_width = w_in.shape[1]
    model_width = width * Y * ZH
    near = lax.all_gather(
        jnp.concatenate([patches, out_grad], axis=1), "zl", axis=0, tiled=True
    )
    cotangent = near[:, width:]
    below, above = shift(cotangent, "x", X, 1), shift(cotangent, "x", X, -1)
    values = near[:, :width].astype(F32)
    image = jnp.sum(norm_gain[:, None] * w_in.astype(F32), axis=0)
    sums = jnp.sum(
        to_all(
            jnp.concatenate([jnp.sum(values, axis=1), jnp.sum(values * values, axis=1), image]),
            ROW,
        ),
        axis=0,
    )
    count = near.shape[0]
    average = (sums[:count] / model_width)[:, None]
    squares = (sums[count : 2 * count] / model_width)[:, None]
    image = sums[2 * count :]
    inverse = lax.rsqrt(squares - average * average + 1e-06)
    centred = (values - average) * inverse
    normed, below, above = lax.optimization_barrier(
        ((centred * norm_gain).astype(BF16), below, above)
    )
    half = count // 2
    place = lax.axis_index("x")

    def panel(own, below, above, far):
        whole = jnp.zeros((X * count, width), BF16)
        for by, block in ((0, own), (-1, below), (1, above), (2, far)):
            start = ((place + (by + X)) & (X - 1)) * count
            whole = lax.dynamic_update_slice(
                whole, block, (start, 0), allow_negative_indices=False
            )
        return whole

    up = shift(jnp.concatenate([normed, below[:half]], axis=0), "x", X, 1)
    down = shift(jnp.concatenate([normed, above[half:]], axis=0), "x", X, -1)
    normed_panel = panel(normed, up[:count], down[:count], shift(normed, "x", X, 2))
    far = jnp.concatenate([up[count:], down[count:]], axis=0)
    cotangent = panel(cotangent, below, above, far)
    own = lax.axis_index("zl") * tokens
    centred, inverse = (
        lax.dynamic_slice(
            a, (own, 0), (tokens, a.shape[1]), allow_negative_indices=False
        )
        for a in (centred, inverse)
    )
    pre_part = jnp.dot(normed_panel, w_in, preferred_element_type=F32).astype(BF16)
    hid_part = contract_last(cotangent, w_out).astype(BF16)
    rows = cotangent.shape[0] // Y

    def part(place):
        return jnp.concatenate(
            [
                lax.dynamic_slice(
                    a, (place * rows, 0), (rows, hidden_width), allow_negative_indices=False
                )
                for a in (pre_part, hid_part)
            ],
            axis=1,
        )

    half_sum = scatter_y(part).astype(BF16)
    total = add(half_sum, shift(half_sum, "zh", ZH, 1))
    pre, hid_grad = total[:, :hidden_width], total[:, hidden_width:]
    activation, slope = jax.vjp(jax.nn.gelu, pre)
    pre_grad = slope(hid_grad)[0].astype(BF16)
    first = jnp.sum(pre_grad.astype(F32) * image, axis=1, keepdims=True)
    second = jnp.sum(pre_grad.astype(F32) * pre, axis=1, keepdims=True)
    lane = lax.broadcasted_iota(jnp.int32, (rows, LANES), 1)
    shares = jnp.zeros((rows, LANES), BF16)
    for place, term in enumerate(split_high_low(first) + split_high_low(second)):
        shares = jnp.where(lane == place, term, shares)
    hidden_panel, pre_grad_panel, shares = gather_ring(
        [activation.astype(BF16), pre_grad, shares], "y", Y
    )
    branch_part = jnp.dot(hidden_panel, w_out, preferred_element_type=F32).astype(BF16)
    normed_grad_part = contract_last(pre_grad_panel, w_in)
    gain_part = jnp.sum(normed_grad_part * normed_panel.astype(F32), axis=0)
    sent = row_major(
        jnp.concatenate([branch_part, normed_grad_part.astype(BF16), shares], axis=1)
    )
    back, gain_sum = scatter(sent, gain_part, "x", X)
    back, gain_sum = scatter(back.astype(BF16), gain_sum, "zl", ZL)
    branch = back[:, :width].astype(BF16)
    normed_grad = back[:, width : 2 * width]
    rest = back[:, 2 * width :]
    lane = lax.broadcasted_iota(jnp.int32, rest.shape, 1)
    first = jnp.sum(jnp.where(lane < 2, rest, 0), axis=1, keepdims=True) / model_width
    second = jnp.sum(jnp.where(lane >= 2, rest, 0), axis=1, keepdims=True) / model_width
    grad_gain = (gain_sum + shift(gain_sum, "dp", 2, 1)) / norm_gain
    grad_patches = inverse * (normed_grad * norm_gain - first - centred * second)
    local_in = contract_tokens(normed_panel, pre_grad_panel).astype(BF16)
    local_out = contract_tokens(hidden_panel, cotangent).astype(BF16)
    grad_w_in = add(local_in, shift(local_in, "dp", 2, 1))
    grad_w_out = add(local_out, shift(local_out, "dp", 2, 1))
    return (branch, grad_patches.astype(BF16), grad_w_in, grad_w_out, grad_gain)


def solution(mesh):
    fine = Mesh(mesh.devices.reshape(-1, Y, ZH, X, ZL), ("dp",) + ROW + COL)
    return jax.shard_map(
        shards,
        mesh=fine,
        in_specs=(
            P(("dp",) + COL, ROW),
            P(ROW),
            P(ROW, COL),
            P(COL, ROW),
            P(("dp",) + COL, ROW),
        ),
        out_specs=(
            P(("dp",) + COL, ROW),
            P(("dp",) + COL, ROW),
            P(ROW, COL),
            P(COL, ROW),
            P(ROW),
        ),
        check_vma=False,
    )
```

```python
import jax
import jax.numpy as jnp
from jax import lax
from jax.experimental.layout import Layout, with_layout_constraint
from jax.sharding import Mesh, PartitionSpec as P

Y, ZH, X, ZL = 8, 2, 4, 4
ROW = ("y", "zh")
COL = ("x", "zl")
F32, BF16 = jnp.float32, jnp.bfloat16
LANES = 128


def contract_tokens(left, right):
    return lax.dot_general(
        left, right, (((0,), (0,)), ((), ())), preferred_element_type=F32
    )


def contract_last(left, right):
    return lax.dot_general(
        left, right, (((1,), (1,)), ((), ())), preferred_element_type=F32
    )


def shift(values, axis, size, by):
    return lax.ppermute(values, axis, [(i, (i + by) % size) for i in range(size)])


def row_major(values):
    return with_layout_constraint(values, Layout((0, 1)))


def add(*terms):
    total = terms[0].astype(F32)
    for term in terms[1:]:
        total = total + term.astype(F32)
    return total


def to_all(values, axes):
    count = {ROW: Y * ZH, COL: X * ZL}[axes]
    copies = jnp.broadcast_to(values, (count,) + values.shape)
    return lax.all_to_all(copies, axes, 0, 0, tiled=True)


def split_high_low(values):
    high = lax.reduce_precision(values, 8, 7)
    return high.astype(BF16), (values - high).astype(BF16)


def scatter_y(part):
    me = lax.axis_index("y")

    def at(by):
        return part((me + (by + Y)) & (Y - 1))

    far = at(4)
    half = far.shape[0] // 2
    up, down = shift(at(3), "y", Y, 1), shift(at(-3), "y", Y, -1)
    up_far, down_far = shift(far[:half], "y", Y, 2), shift(far[half:], "y", Y, -2)
    above, below = at(2), at(-2)
    up = jnp.concatenate(
        [
            add(up[:half], up_far, above[:half]).astype(BF16),
            add(up[half:], above[half:]).astype(BF16),
        ],
        axis=0,
    )
    down = jnp.concatenate(
        [
            add(down[:half], below[:half]).astype(BF16),
            add(down[half:], down_far, below[half:]).astype(BF16),
        ],
        axis=0,
    )
    up, down = shift(up, "y", Y, 1), shift(down, "y", Y, -1)
    up, down = add(up, at(1)).astype(BF16), add(down, at(-1)).astype(BF16)
    up, down = shift(up, "y", Y, 1), shift(down, "y", Y, -1)
    return add(at(0), up, down)


def gather_ring(blocks, axis, size):
    me, rows = lax.axis_index(axis), blocks[0].shape[0]
    half = rows // 2
    panels = [jnp.zeros((size * rows, b.shape[1]), b.dtype) for b in blocks]
    edges = [0]
    for b in blocks:
        edges.append(edges[-1] + b.shape[1])

    def put(panels, values, by, offset=0):
        start = ((me + (by + size)) & (size - 1)) * rows + offset
        return [
            lax.dynamic_update_slice(
                panel, values[:, low:high], (start, 0), allow_negative_indices=False
            )
            for panel, low, high in zip(panels, edges[:-1], edges[1:])
        ]

    block = jnp.concatenate(blocks, axis=1)
    panels = put(panels, block, 0)
    below = above = block
    for by in range(1, size // 2):
        below, above = shift(below, axis, size, 1), shift(above, axis, size, -1)
        panels = put(put(panels, below, -by), above, by)
    panels = put(panels, shift(below[:half], axis, size, 1), size // 2)
    return put(panels, shift(above[half:], axis, size, -1), size // 2, half)


def scatter(sent, vector, axis, size):
    width, long = sent.shape[1], vector.shape[0]
    rows = [jnp.pad(term, (0, width - long))[None] for term in split_high_low(vector)]
    rows = jnp.concatenate(rows + [jnp.zeros((6, width), BF16)], axis=0)
    parts = jnp.concatenate(
        [sent.reshape(size, -1, width), jnp.broadcast_to(rows, (size, 8, width))], axis=1
    )
    back = lax.all_to_all(parts, axis, 0, 0, tiled=True)
    rows = back.shape[1] - 8
    high, low = jnp.sum(back[:, rows : rows + 2, :long].astype(F32), axis=0)
    return jnp.sum(back[:, :rows].astype(F32), axis=0), high + low


def shards(patches, norm_gain, w_in, w_out, out_grad):
    tokens, width = patches.shape
    hidden_width = w_in.shape[1]
    model_width = width * Y * ZH
    near = lax.all_gather(
        jnp.concatenate([patches, out_grad], axis=1), "zl", axis=0, tiled=True
    )
    cotangent = near[:, width:]
    below, above = shift(cotangent, "x", X, 1), shift(cotangent, "x", X, -1)
    values = near[:, :width].astype(F32)
    image = jnp.sum(norm_gain[:, None] * w_in.astype(F32), axis=0)
    sums = jnp.sum(
        to_all(
            jnp.concatenate([jnp.sum(values, axis=1), jnp.sum(values * values, axis=1), image]),
            ROW,
        ),
        axis=0,
    )
    count = near.shape[0]
    average = (sums[:count] / model_width)[:, None]
    squares = (sums[count : 2 * count] / model_width)[:, None]
    image = sums[2 * count :]
    inverse = lax.rsqrt(squares - average * average + 1e-06)
    centred = (values - average) * inverse
    normed, below, above = lax.optimization_barrier(
        ((centred * norm_gain).astype(BF16), below, above)
    )
    half = count // 2
    place = lax.axis_index("x")

    def panel(own, below, above, far):
        whole = jnp.zeros((X * count, width), BF16)
        for by, block in ((0, own), (-1, below), (1, above), (2, far)):
            start = ((place + (by + X)) & (X - 1)) * count
            whole = lax.dynamic_update_slice(
                whole, block, (start, 0), allow_negative_indices=False
            )
        return whole

    up = shift(jnp.concatenate([normed, below[:half]], axis=0), "x", X, 1)
    down = shift(jnp.concatenate([normed, above[half:]], axis=0), "x", X, -1)
    normed_panel = panel(normed, up[:count], down[:count], shift(normed, "x", X, 2))
    far = jnp.concatenate([up[count:], down[count:]], axis=0)
    cotangent = panel(cotangent, below, above, far)
    own = lax.axis_index("zl") * tokens
    centred, inverse = (
        lax.dynamic_slice(
            a, (own, 0), (tokens, a.shape[1]), allow_negative_indices=False
        )
        for a in (centred, inverse)
    )
    pre_part = jnp.dot(normed_panel, w_in, preferred_element_type=F32).astype(BF16)
    hid_part = contract_last(cotangent, w_out).astype(BF16)
    rows = cotangent.shape[0] // Y

    def part(place):
        return jnp.concatenate(
            [
                lax.dynamic_slice(
                    a, (place * rows, 0), (rows, hidden_width), allow_negative_indices=False
                )
                for a in (pre_part, hid_part)
            ],
            axis=1,
        )

    half_sum = scatter_y(part).astype(BF16)
    total = add(half_sum, shift(half_sum, "zh", ZH, 1))
    pre, hid_grad = total[:, :hidden_width], total[:, hidden_width:]
    activation, slope = jax.vjp(jax.nn.gelu, pre)
    pre_grad = slope(hid_grad)[0].astype(BF16)
    first = jnp.sum(pre_grad.astype(F32) * image, axis=1, keepdims=True)
    second = jnp.sum(pre_grad.astype(F32) * pre, axis=1, keepdims=True)
    lane = lax.broadcasted_iota(jnp.int32, (rows, LANES), 1)
    shares = jnp.zeros((rows, LANES), BF16)
    for place, term in enumerate(split_high_low(first) + split_high_low(second)):
        shares = jnp.where(lane == place, term, shares)
    hidden_panel = lax.all_gather(activation.astype(BF16), "y", axis=0, tiled=True)
    pre_grad_panel, shares = gather_ring([pre_grad, shares], "y", Y)
    branch_part = jnp.dot(hidden_panel, w_out, preferred_element_type=F32).astype(BF16)
    normed_grad_part = contract_last(pre_grad_panel, w_in)
    gain_part = jnp.sum(normed_grad_part * normed_panel.astype(F32), axis=0)
    sent = row_major(jnp.concatenate([normed_grad_part.astype(BF16), shares], axis=1))
    back, gain_sum = scatter(sent, gain_part, "x", X)
    branch = lax.all_to_all(branch_part.reshape(X, -1, width), "x", 0, 0, tiled=True)
    branch = jnp.sum(branch.astype(F32), axis=0)
    back = jnp.concatenate([branch, back], axis=1).astype(BF16)
    back, gain_sum = scatter(back, gain_sum, "zl", ZL)
    branch = back[:, :width].astype(BF16)
    normed_grad = back[:, width : 2 * width]
    rest = back[:, 2 * width :]
    lane = lax.broadcasted_iota(jnp.int32, rest.shape, 1)
    first = jnp.sum(jnp.where(lane < 2, rest, 0), axis=1, keepdims=True) / model_width
    second = jnp.sum(jnp.where(lane >= 2, rest, 0), axis=1, keepdims=True) / model_width
    grad_gain = (gain_sum + shift(gain_sum, "dp", 2, 1)) / norm_gain
    grad_patches = inverse * (normed_grad * norm_gain - first - centred * second)
    local_in = contract_tokens(normed_panel, pre_grad_panel).astype(BF16)
    local_out = contract_tokens(hidden_panel, cotangent).astype(BF16)
    grad_w_in = add(local_in, shift(local_in, "dp", 2, 1))
    grad_w_out = add(local_out, shift(local_out, "dp", 2, 1))
    return (branch, grad_patches.astype(BF16), grad_w_in, grad_w_out, grad_gain)


def solution(mesh):
    fine = Mesh(mesh.devices.reshape(-1, Y, ZH, X, ZL), ("dp",) + ROW + COL)
    return jax.shard_map(
        shards,
        mesh=fine,
        in_specs=(
            P(("dp",) + COL, ROW),
            P(ROW),
            P(ROW, COL),
            P(COL, ROW),
            P(("dp",) + COL, ROW),
        ),
        out_specs=(
            P(("dp",) + COL, ROW),
            P(("dp",) + COL, ROW),
            P(ROW, COL),
            P(COL, ROW),
            P(ROW),
        ),
        check_vma=False,
    )
```

```python
import jax
import jax.numpy as jnp
from jax import lax
from jax.experimental.layout import Layout, with_layout_constraint
from jax.sharding import Mesh, PartitionSpec as P

Y, ZH, X, ZL = 8, 2, 4, 4
ROW = ("y", "zh")
COL = ("x", "zl")
F32, BF16 = jnp.float32, jnp.bfloat16
LANES = 128


def contract_tokens(left, right):
    return lax.dot_general(
        left, right, (((0,), (0,)), ((), ())), preferred_element_type=F32
    )


def contract_last(left, right):
    return lax.dot_general(
        left, right, (((1,), (1,)), ((), ())), preferred_element_type=F32
    )


def shift(values, axis, size, by):
    return lax.ppermute(values, axis, [(i, (i + by) % size) for i in range(size)])


def row_major(values):
    return with_layout_constraint(values, Layout((0, 1)))


def add(*terms):
    total = terms[0].astype(F32)
    for term in terms[1:]:
        total = total + term.astype(F32)
    return total


def to_all(values, axes):
    count = {ROW: Y * ZH, COL: X * ZL}[axes]
    copies = jnp.broadcast_to(values, (count,) + values.shape)
    return lax.all_to_all(copies, axes, 0, 0, tiled=True)


def split_high_low(values):
    high = lax.reduce_precision(values, 8, 7)
    return high.astype(BF16), (values - high).astype(BF16)


def scatter_y(part):
    me = lax.axis_index("y")

    def at(by):
        return part((me + (by + Y)) & (Y - 1))

    far = at(4)
    half = far.shape[0] // 2
    up, down = shift(at(3), "y", Y, 1), shift(at(-3), "y", Y, -1)
    up_far, down_far = shift(far[:half], "y", Y, 2), shift(far[half:], "y", Y, -2)
    above, below = at(2), at(-2)
    up = jnp.concatenate(
        [
            add(up[:half], up_far, above[:half]).astype(BF16),
            add(up[half:], above[half:]).astype(BF16),
        ],
        axis=0,
    )
    down = jnp.concatenate(
        [
            add(down[:half], below[:half]).astype(BF16),
            add(down[half:], down_far, below[half:]).astype(BF16),
        ],
        axis=0,
    )
    up, down = shift(up, "y", Y, 1), shift(down, "y", Y, -1)
    up, down = add(up, at(1)).astype(BF16), add(down, at(-1)).astype(BF16)
    up, down = shift(up, "y", Y, 1), shift(down, "y", Y, -1)
    return add(at(0), up, down)


def gather_ring(blocks, axis, size):
    me, rows = lax.axis_index(axis), blocks[0].shape[0]
    half = rows // 2
    panels = [jnp.zeros((size * rows, b.shape[1]), b.dtype) for b in blocks]
    edges = [0]
    for b in blocks:
        edges.append(edges[-1] + b.shape[1])

    def put(panels, values, by, offset=0):
        start = ((me + (by + size)) & (size - 1)) * rows + offset
        return [
            lax.dynamic_update_slice(
                panel, values[:, low:high], (start, 0), allow_negative_indices=False
            )
            for panel, low, high in zip(panels, edges[:-1], edges[1:])
        ]

    block = jnp.concatenate(blocks, axis=1)
    panels = put(panels, block, 0)
    below = above = block
    for by in range(1, size // 2):
        below, above = shift(below, axis, size, 1), shift(above, axis, size, -1)
        panels = put(put(panels, below, -by), above, by)
    panels = put(panels, shift(below[:half], axis, size, 1), size // 2)
    return put(panels, shift(above[half:], axis, size, -1), size // 2, half)


def scatter(sent, vector, axis, size):
    width, long = sent.shape[1], vector.shape[0]
    row = jnp.pad(jnp.concatenate(split_high_low(vector)), (0, width - 2 * long))
    parts = jnp.concatenate(
        [sent.reshape(size, -1, width), jnp.broadcast_to(row, (size, 8, width))], axis=1
    )
    back = lax.all_to_all(parts, axis, 0, 0, tiled=True)
    rows = back.shape[1] - 8
    row = jnp.sum(back[:, rows].astype(F32), axis=0)
    total = jnp.sum(back[:, :rows].astype(F32), axis=0)
    return total, row[:long] + row[long : 2 * long]


def shards(patches, norm_gain, w_in, w_out, out_grad):
    tokens, width = patches.shape
    hidden_width = w_in.shape[1]
    model_width = width * Y * ZH
    near = lax.all_gather(
        jnp.concatenate([patches, out_grad], axis=1), "zl", axis=0, tiled=True
    )
    cotangent = near[:, width:]
    below, above = shift(cotangent, "x", X, 1), shift(cotangent, "x", X, -1)
    values = near[:, :width].astype(F32)
    image = jnp.sum(norm_gain[:, None] * w_in.astype(F32), axis=0)
    sums = jnp.sum(
        to_all(
            jnp.concatenate([jnp.sum(values, axis=1), jnp.sum(values * values, axis=1), image]),
            ROW,
        ),
        axis=0,
    )
    count = near.shape[0]
    average = (sums[:count] / model_width)[:, None]
    squares = (sums[count : 2 * count] / model_width)[:, None]
    image = sums[2 * count :]
    inverse = lax.rsqrt(squares - average * average + 1e-06)
    centred = (values - average) * inverse
    normed, below, above = lax.optimization_barrier(
        ((centred * norm_gain).astype(BF16), below, above)
    )
    half = count // 2
    place = lax.axis_index("x")

    def panel(own, below, above, far):
        whole = jnp.zeros((X * count, width), BF16)
        for by, block in ((0, own), (-1, below), (1, above), (2, far)):
            start = ((place + (by + X)) & (X - 1)) * count
            whole = lax.dynamic_update_slice(
                whole, block, (start, 0), allow_negative_indices=False
            )
        return whole

    up = shift(jnp.concatenate([normed, below[:half]], axis=0), "x", X, 1)
    down = shift(jnp.concatenate([normed, above[half:]], axis=0), "x", X, -1)
    normed_panel = panel(normed, up[:count], down[:count], shift(normed, "x", X, 2))
    far = jnp.concatenate([up[count:], down[count:]], axis=0)
    cotangent = panel(cotangent, below, above, far)
    own = lax.axis_index("zl") * tokens
    centred, inverse = (
        lax.dynamic_slice(
            a, (own, 0), (tokens, a.shape[1]), allow_negative_indices=False
        )
        for a in (centred, inverse)
    )
    pre_part = jnp.dot(normed_panel, w_in, preferred_element_type=F32).astype(BF16)
    hid_part = contract_last(cotangent, w_out).astype(BF16)
    rows = cotangent.shape[0] // Y

    def part(place):
        return jnp.concatenate(
            [
                lax.dynamic_slice(
                    a, (place * rows, 0), (rows, hidden_width), allow_negative_indices=False
                )
                for a in (pre_part, hid_part)
            ],
            axis=1,
        )

    half_sum = scatter_y(part).astype(BF16)
    total = add(half_sum, shift(half_sum, "zh", ZH, 1))
    pre, hid_grad = total[:, :hidden_width], total[:, hidden_width:]
    activation, slope = jax.vjp(jax.nn.gelu, pre)
    pre_grad = slope(hid_grad)[0].astype(BF16)
    first = jnp.sum(pre_grad.astype(F32) * image, axis=1, keepdims=True)
    second = jnp.sum(pre_grad.astype(F32) * pre, axis=1, keepdims=True)
    lane = lax.broadcasted_iota(jnp.int32, (rows, LANES), 1)
    shares = jnp.zeros((rows, LANES), BF16)
    for place, term in enumerate(split_high_low(first) + split_high_low(second)):
        shares = jnp.where(lane == place, term, shares)
    hidden_panel, pre_grad_panel, shares = gather_ring(
        [activation.astype(BF16), pre_grad, shares], "y", Y
    )
    branch_part = jnp.dot(hidden_panel, w_out, preferred_element_type=F32).astype(BF16)
    normed_grad_part = contract_last(pre_grad_panel, w_in)
    gain_part = jnp.sum(normed_grad_part * normed_panel.astype(F32), axis=0)
    sent = row_major(
        jnp.concatenate([branch_part, normed_grad_part.astype(BF16), shares], axis=1)
    )
    back, gain_sum = scatter(sent, gain_part, "x", X)
    back, gain_sum = scatter(back.astype(BF16), gain_sum, "zl", ZL)
    branch = back[:, :width].astype(BF16)
    normed_grad = back[:, width : 2 * width]
    rest = back[:, 2 * width :]
    lane = lax.broadcasted_iota(jnp.int32, rest.shape, 1)
    first = jnp.sum(jnp.where(lane < 2, rest, 0), axis=1, keepdims=True) / model_width
    second = jnp.sum(jnp.where(lane >= 2, rest, 0), axis=1, keepdims=True) / model_width
    grad_gain = (gain_sum + shift(gain_sum, "dp", 2, 1)) / norm_gain
    grad_patches = inverse * (normed_grad * norm_gain - first - centred * second)
    local_in = contract_tokens(normed_panel, pre_grad_panel).astype(BF16)
    local_out = contract_tokens(hidden_panel, cotangent).astype(BF16)
    grad_w_in = add(local_in, shift(local_in, "dp", 2, 1))
    grad_w_out = add(local_out, shift(local_out, "dp", 2, 1))
    return (branch, grad_patches.astype(BF16), grad_w_in, grad_w_out, grad_gain)


def solution(mesh):
    fine = Mesh(mesh.devices.reshape(-1, Y, ZH, X, ZL), ("dp",) + ROW + COL)
    return jax.shard_map(
        shards,
        mesh=fine,
        in_specs=(
            P(("dp",) + COL, ROW),
            P(ROW),
            P(ROW, COL),
            P(COL, ROW),
            P(("dp",) + COL, ROW),
        ),
        out_specs=(
            P(("dp",) + COL, ROW),
            P(("dp",) + COL, ROW),
            P(ROW, COL),
            P(COL, ROW),
            P(ROW),
        ),
        check_vma=False,
    )
```

```python
import jax
import jax.numpy as jnp
from jax import lax
from jax.experimental.layout import Layout, with_layout_constraint
from jax.sharding import Mesh, PartitionSpec as P

Y, ZH, X, ZL = 8, 2, 4, 4
ROW = ("y", "zh")
COL = ("x", "zl")
F32, BF16 = jnp.float32, jnp.bfloat16
LANES = 128


def contract_tokens(left, right):
    return lax.dot_general(
        left, right, (((0,), (0,)), ((), ())), preferred_element_type=F32
    )


def contract_last(left, right):
    return lax.dot_general(
        left, right, (((1,), (1,)), ((), ())), preferred_element_type=F32
    )


def shift(values, axis, size, by):
    return lax.ppermute(values, axis, [(i, (i + by) % size) for i in range(size)])


def row_major(values):
    return with_layout_constraint(values, Layout((0, 1)))


def add(*terms):
    total = terms[0].astype(F32)
    for term in terms[1:]:
        total = total + term.astype(F32)
    return total


def to_all(values, axes):
    count = {ROW: Y * ZH, COL: X * ZL}[axes]
    copies = jnp.broadcast_to(values, (count,) + values.shape)
    return lax.all_to_all(copies, axes, 0, 0, tiled=True)


def split_high_low(values):
    high = lax.reduce_precision(values, 8, 7)
    return high.astype(BF16), (values - high).astype(BF16)


def scatter_y(part):
    me = lax.axis_index("y")

    def at(by):
        return part((me + (by + Y)) & (Y - 1))

    far = at(4)
    half = far.shape[0] // 2
    up, down = shift(at(3), "y", Y, 1), shift(at(-3), "y", Y, -1)
    up_far, down_far = shift(far[:half], "y", Y, 2), shift(far[half:], "y", Y, -2)
    above, below = at(2), at(-2)
    up = jnp.concatenate(
        [
            add(up[:half], up_far, above[:half]).astype(BF16),
            add(up[half:], above[half:]).astype(BF16),
        ],
        axis=0,
    )
    down = jnp.concatenate(
        [
            add(down[:half], below[:half]).astype(BF16),
            add(down[half:], down_far, below[half:]).astype(BF16),
        ],
        axis=0,
    )
    near = shift(at(1), "y", Y, 1), shift(at(-1), "y", Y, -1)
    up, down = shift(up, "y", Y, 2), shift(down, "y", Y, -2)
    return add(at(0), up, down, *near)


def gather_ring(blocks, axis, size):
    me, rows = lax.axis_index(axis), blocks[0].shape[0]
    half = rows // 2
    panels = [jnp.zeros((size * rows, b.shape[1]), b.dtype) for b in blocks]
    edges = [0]
    for b in blocks:
        edges.append(edges[-1] + b.shape[1])

    def put(panels, values, by, offset=0):
        start = ((me + (by + size)) & (size - 1)) * rows + offset
        return [
            lax.dynamic_update_slice(
                panel, values[:, low:high], (start, 0), allow_negative_indices=False
            )
            for panel, low, high in zip(panels, edges[:-1], edges[1:])
        ]

    block = jnp.concatenate(blocks, axis=1)
    panels = put(panels, block, 0)
    below = above = block
    for by in range(1, size // 2):
        below, above = shift(below, axis, size, 1), shift(above, axis, size, -1)
        panels = put(put(panels, below, -by), above, by)
    panels = put(panels, shift(below[:half], axis, size, 1), size // 2)
    return put(panels, shift(above[half:], axis, size, -1), size // 2, half)


def scatter(sent, vector, axis, size):
    width, long = sent.shape[1], vector.shape[0]
    row = jnp.pad(jnp.concatenate(split_high_low(vector)), (0, width - 2 * long))
    parts = jnp.concatenate(
        [sent.reshape(size, -1, width), jnp.broadcast_to(row, (size, 8, width))], axis=1
    )
    back = lax.all_to_all(parts, axis, 0, 0, tiled=True)
    rows = back.shape[1] - 8
    row = jnp.sum(back[:, rows].astype(F32), axis=0)
    total = jnp.sum(back[:, :rows].astype(F32), axis=0)
    return total, row[:long] + row[long : 2 * long]


def shards(patches, norm_gain, w_in, w_out, out_grad):
    tokens, width = patches.shape
    hidden_width = w_in.shape[1]
    model_width = width * Y * ZH
    near = lax.all_gather(
        jnp.concatenate([patches, out_grad], axis=1), "zl", axis=0, tiled=True
    )
    cotangent = near[:, width:]
    below, above = shift(cotangent, "x", X, 1), shift(cotangent, "x", X, -1)
    values = near[:, :width].astype(F32)
    image = jnp.sum(norm_gain[:, None] * w_in.astype(F32), axis=0)
    sums = jnp.sum(
        to_all(
            jnp.concatenate([jnp.sum(values, axis=1), jnp.sum(values * values, axis=1), image]),
            ROW,
        ),
        axis=0,
    )
    count = near.shape[0]
    average = (sums[:count] / model_width)[:, None]
    squares = (sums[count : 2 * count] / model_width)[:, None]
    image = sums[2 * count :]
    inverse = lax.rsqrt(squares - average * average + 1e-06)
    centred = (values - average) * inverse
    normed, below, above = lax.optimization_barrier(
        ((centred * norm_gain).astype(BF16), below, above)
    )
    half = count // 2
    place = lax.axis_index("x")

    def panel(own, below, above, far):
        whole = jnp.zeros((X * count, width), BF16)
        for by, block in ((0, own), (-1, below), (1, above), (2, far)):
            start = ((place + (by + X)) & (X - 1)) * count
            whole = lax.dynamic_update_slice(
                whole, block, (start, 0), allow_negative_indices=False
            )
        return whole

    up = shift(jnp.concatenate([normed, below[:half]], axis=0), "x", X, 1)
    down = shift(jnp.concatenate([normed, above[half:]], axis=0), "x", X, -1)
    normed_panel = panel(normed, up[:count], down[:count], shift(normed, "x", X, 2))
    far = jnp.concatenate([up[count:], down[count:]], axis=0)
    cotangent = panel(cotangent, below, above, far)
    own = lax.axis_index("zl") * tokens
    centred, inverse = (
        lax.dynamic_slice(
            a, (own, 0), (tokens, a.shape[1]), allow_negative_indices=False
        )
        for a in (centred, inverse)
    )
    pre_part = jnp.dot(normed_panel, w_in, preferred_element_type=F32).astype(BF16)
    hid_part = contract_last(cotangent, w_out).astype(BF16)
    rows = cotangent.shape[0] // Y

    def part(place):
        return jnp.concatenate(
            [
                lax.dynamic_slice(
                    a, (place * rows, 0), (rows, hidden_width), allow_negative_indices=False
                )
                for a in (pre_part, hid_part)
            ],
            axis=1,
        )

    half_sum = scatter_y(part).astype(BF16)
    total = add(half_sum, shift(half_sum, "zh", ZH, 1))
    pre, hid_grad = total[:, :hidden_width], total[:, hidden_width:]
    activation, slope = jax.vjp(jax.nn.gelu, pre)
    pre_grad = slope(hid_grad)[0].astype(BF16)
    first = jnp.sum(pre_grad.astype(F32) * image, axis=1, keepdims=True)
    second = jnp.sum(pre_grad.astype(F32) * pre, axis=1, keepdims=True)
    lane = lax.broadcasted_iota(jnp.int32, (rows, LANES), 1)
    shares = jnp.zeros((rows, LANES), BF16)
    for place, term in enumerate(split_high_low(first) + split_high_low(second)):
        shares = jnp.where(lane == place, term, shares)
    hidden_panel, pre_grad_panel, shares = gather_ring(
        [activation.astype(BF16), pre_grad, shares], "y", Y
    )
    branch_part = jnp.dot(hidden_panel, w_out, preferred_element_type=F32).astype(BF16)
    normed_grad_part = contract_last(pre_grad_panel, w_in)
    gain_part = jnp.sum(normed_grad_part * normed_panel.astype(F32), axis=0)
    sent = row_major(
        jnp.concatenate([branch_part, normed_grad_part.astype(BF16), shares], axis=1)
    )
    back, gain_sum = scatter(sent, gain_part, "x", X)
    back, gain_sum = scatter(back.astype(BF16), gain_sum, "zl", ZL)
    branch = back[:, :width].astype(BF16)
    normed_grad = back[:, width : 2 * width]
    rest = back[:, 2 * width :]
    lane = lax.broadcasted_iota(jnp.int32, rest.shape, 1)
    first = jnp.sum(jnp.where(lane < 2, rest, 0), axis=1, keepdims=True) / model_width
    second = jnp.sum(jnp.where(lane >= 2, rest, 0), axis=1, keepdims=True) / model_width
    grad_gain = (gain_sum + shift(gain_sum, "dp", 2, 1)) / norm_gain
    grad_patches = inverse * (normed_grad * norm_gain - first - centred * second)
    local_in = contract_tokens(normed_panel, pre_grad_panel).astype(BF16)
    local_out = contract_tokens(hidden_panel, cotangent).astype(BF16)
    grad_w_in = add(local_in, shift(local_in, "dp", 2, 1))
    grad_w_out = add(local_out, shift(local_out, "dp", 2, 1))
    return (branch, grad_patches.astype(BF16), grad_w_in, grad_w_out, grad_gain)


def solution(mesh):
    fine = Mesh(mesh.devices.reshape(-1, Y, ZH, X, ZL), ("dp",) + ROW + COL)
    return jax.shard_map(
        shards,
        mesh=fine,
        in_specs=(
            P(("dp",) + COL, ROW),
            P(ROW),
            P(ROW, COL),
            P(COL, ROW),
            P(("dp",) + COL, ROW),
        ),
        out_specs=(
            P(("dp",) + COL, ROW),
            P(("dp",) + COL, ROW),
            P(ROW, COL),
            P(COL, ROW),
            P(ROW),
        ),
        check_vma=False,
    )
```

```python
import jax
import jax.numpy as jnp
from jax import lax
from jax.experimental.layout import Layout, with_layout_constraint
from jax.sharding import Mesh, PartitionSpec as P

Y, ZH, X, ZL = 8, 2, 4, 4
ROW = ("y", "zh")
COL = ("x", "zl")
F32, BF16 = jnp.float32, jnp.bfloat16
LANES = 128


def contract_tokens(left, right):
    return lax.dot_general(
        left, right, (((0,), (0,)), ((), ())), preferred_element_type=F32
    )


def contract_last(left, right):
    return lax.dot_general(
        left, right, (((1,), (1,)), ((), ())), preferred_element_type=F32
    )


def shift(values, axis, size, by):
    return lax.ppermute(values, axis, [(i, (i + by) % size) for i in range(size)])


def row_major(values):
    return with_layout_constraint(values, Layout((0, 1)))


def add(*terms):
    total = terms[0].astype(F32)
    for term in terms[1:]:
        total = total + term.astype(F32)
    return total


def to_all(values, axes):
    count = {ROW: Y * ZH, COL: X * ZL}[axes]
    copies = jnp.broadcast_to(values, (count,) + values.shape)
    return lax.all_to_all(copies, axes, 0, 0, tiled=True)


def split_high_low(values):
    high = lax.reduce_precision(values, 8, 7)
    return high.astype(BF16), (values - high).astype(BF16)


def scatter_y(part):
    me = lax.axis_index("y")

    def at(by):
        return part((me + (by + Y)) & (Y - 1))

    far = at(4)
    half = far.shape[0] // 2
    up, down = shift(at(3), "y", Y, 1), shift(at(-3), "y", Y, -1)
    up_far, down_far = shift(far[:half], "y", Y, 2), shift(far[half:], "y", Y, -2)
    above, below = at(2), at(-2)
    up = jnp.concatenate(
        [
            add(up[:half], up_far, above[:half]).astype(BF16),
            add(up[half:], above[half:]).astype(BF16),
        ],
        axis=0,
    )
    down = jnp.concatenate(
        [
            add(down[:half], below[:half]).astype(BF16),
            add(down[half:], down_far, below[half:]).astype(BF16),
        ],
        axis=0,
    )
    up, down, *near = lax.optimization_barrier((up, down, at(1), at(-1)))
    near = shift(near[0], "y", Y, 1), shift(near[1], "y", Y, -1)
    up, down = shift(up, "y", Y, 2), shift(down, "y", Y, -2)
    return add(at(0), up, down, *near)


def gather_ring(blocks, axis, size):
    me, rows = lax.axis_index(axis), blocks[0].shape[0]
    half = rows // 2
    panels = [jnp.zeros((size * rows, b.shape[1]), b.dtype) for b in blocks]
    edges = [0]
    for b in blocks:
        edges.append(edges[-1] + b.shape[1])

    def put(panels, values, by, offset=0):
        start = ((me + (by + size)) & (size - 1)) * rows + offset
        return [
            lax.dynamic_update_slice(
                panel, values[:, low:high], (start, 0), allow_negative_indices=False
            )
            for panel, low, high in zip(panels, edges[:-1], edges[1:])
        ]

    block = jnp.concatenate(blocks, axis=1)
    panels = put(panels, block, 0)
    below = above = block
    for by in range(1, size // 2):
        below, above = shift(below, axis, size, 1), shift(above, axis, size, -1)
        panels = put(put(panels, below, -by), above, by)
    panels = put(panels, shift(below[:half], axis, size, 1), size // 2)
    return put(panels, shift(above[half:], axis, size, -1), size // 2, half)


def scatter(sent, vector, axis, size):
    width, long = sent.shape[1], vector.shape[0]
    row = jnp.pad(jnp.concatenate(split_high_low(vector)), (0, width - 2 * long))
    parts = jnp.concatenate(
        [sent.reshape(size, -1, width), jnp.broadcast_to(row, (size, 8, width))], axis=1
    )
    back = lax.all_to_all(parts, axis, 0, 0, tiled=True)
    rows = back.shape[1] - 8
    row = jnp.sum(back[:, rows].astype(F32), axis=0)
    total = jnp.sum(back[:, :rows].astype(F32), axis=0)
    return total, row[:long] + row[long : 2 * long]


def shards(patches, norm_gain, w_in, w_out, out_grad):
    tokens, width = patches.shape
    hidden_width = w_in.shape[1]
    model_width = width * Y * ZH
    near = lax.all_gather(
        jnp.concatenate([patches, out_grad], axis=1), "zl", axis=0, tiled=True
    )
    cotangent = near[:, width:]
    below, above = shift(cotangent, "x", X, 1), shift(cotangent, "x", X, -1)
    values = near[:, :width].astype(F32)
    image = jnp.sum(norm_gain[:, None] * w_in.astype(F32), axis=0)
    sums = jnp.sum(
        to_all(
            jnp.concatenate([jnp.sum(values, axis=1), jnp.sum(values * values, axis=1), image]),
            ROW,
        ),
        axis=0,
    )
    count = near.shape[0]
    average = (sums[:count] / model_width)[:, None]
    squares = (sums[count : 2 * count] / model_width)[:, None]
    image = sums[2 * count :]
    inverse = lax.rsqrt(squares - average * average + 1e-06)
    centred = (values - average) * inverse
    normed, below, above = lax.optimization_barrier(
        ((centred * norm_gain).astype(BF16), below, above)
    )
    half = count // 2
    place = lax.axis_index("x")

    def panel(own, below, above, far):
        whole = jnp.zeros((X * count, width), BF16)
        for by, block in ((0, own), (-1, below), (1, above), (2, far)):
            start = ((place + (by + X)) & (X - 1)) * count
            whole = lax.dynamic_update_slice(
                whole, block, (start, 0), allow_negative_indices=False
            )
        return whole

    up = shift(jnp.concatenate([normed, below[:half]], axis=0), "x", X, 1)
    down = shift(jnp.concatenate([normed, above[half:]], axis=0), "x", X, -1)
    normed_panel = panel(normed, up[:count], down[:count], shift(normed, "x", X, 2))
    far = jnp.concatenate([up[count:], down[count:]], axis=0)
    cotangent = panel(cotangent, below, above, far)
    own = lax.axis_index("zl") * tokens
    centred, inverse = (
        lax.dynamic_slice(
            a, (own, 0), (tokens, a.shape[1]), allow_negative_indices=False
        )
        for a in (centred, inverse)
    )
    pre_part = jnp.dot(normed_panel, w_in, preferred_element_type=F32).astype(BF16)
    hid_part = contract_last(cotangent, w_out).astype(BF16)
    rows = cotangent.shape[0] // Y

    def part(place):
        return jnp.concatenate(
            [
                lax.dynamic_slice(
                    a, (place * rows, 0), (rows, hidden_width), allow_negative_indices=False
                )
                for a in (pre_part, hid_part)
            ],
            axis=1,
        )

    half_sum = scatter_y(part).astype(BF16)
    total = add(half_sum, shift(half_sum, "zh", ZH, 1))
    pre, hid_grad = total[:, :hidden_width], total[:, hidden_width:]
    activation, slope = jax.vjp(jax.nn.gelu, pre)
    pre_grad = slope(hid_grad)[0].astype(BF16)
    first = jnp.sum(pre_grad.astype(F32) * image, axis=1, keepdims=True)
    second = jnp.sum(pre_grad.astype(F32) * pre, axis=1, keepdims=True)
    lane = lax.broadcasted_iota(jnp.int32, (rows, LANES), 1)
    shares = jnp.zeros((rows, LANES), BF16)
    for place, term in enumerate(split_high_low(first) + split_high_low(second)):
        shares = jnp.where(lane == place, term, shares)
    hidden_panel, pre_grad_panel, shares = gather_ring(
        [activation.astype(BF16), pre_grad, shares], "y", Y
    )
    branch_part = jnp.dot(hidden_panel, w_out, preferred_element_type=F32).astype(BF16)
    normed_grad_part = contract_last(pre_grad_panel, w_in)
    gain_part = jnp.sum(normed_grad_part * normed_panel.astype(F32), axis=0)
    sent = row_major(
        jnp.concatenate([branch_part, normed_grad_part.astype(BF16), shares], axis=1)
    )
    back, gain_sum = scatter(sent, gain_part, "x", X)
    back, gain_sum = scatter(back.astype(BF16), gain_sum, "zl", ZL)
    branch = back[:, :width].astype(BF16)
    normed_grad = back[:, width : 2 * width]
    rest = back[:, 2 * width :]
    lane = lax.broadcasted_iota(jnp.int32, rest.shape, 1)
    first = jnp.sum(jnp.where(lane < 2, rest, 0), axis=1, keepdims=True) / model_width
    second = jnp.sum(jnp.where(lane >= 2, rest, 0), axis=1, keepdims=True) / model_width
    grad_gain = (gain_sum + shift(gain_sum, "dp", 2, 1)) / norm_gain
    grad_patches = inverse * (normed_grad * norm_gain - first - centred * second)
    local_in = contract_tokens(normed_panel, pre_grad_panel).astype(BF16)
    local_out = contract_tokens(hidden_panel, cotangent).astype(BF16)
    grad_w_in = add(local_in, shift(local_in, "dp", 2, 1))
    grad_w_out = add(local_out, shift(local_out, "dp", 2, 1))
    return (branch, grad_patches.astype(BF16), grad_w_in, grad_w_out, grad_gain)


def solution(mesh):
    fine = Mesh(mesh.devices.reshape(-1, Y, ZH, X, ZL), ("dp",) + ROW + COL)
    return jax.shard_map(
        shards,
        mesh=fine,
        in_specs=(
            P(("dp",) + COL, ROW),
            P(ROW),
            P(ROW, COL),
            P(COL, ROW),
            P(("dp",) + COL, ROW),
        ),
        out_specs=(
            P(("dp",) + COL, ROW),
            P(("dp",) + COL, ROW),
            P(ROW, COL),
            P(COL, ROW),
            P(ROW),
        ),
        check_vma=False,
    )
```
